768 devices in a mesh: rep: 16 (over y, core), own: 48 (over x, z).
Axes of the slice: x: 4, y: 8, z: 12, core: 2. Of those that a mesh axis runs over, the one named last changes fastest.
Arguments:
- grad_partial: bfloat16 [16, 48, 2, 32, 8192], P('rep', 'own'), may hold values from -0.4375 to 0.4375
- owner: int32 [6, 16], replicated, may hold values from 0 to 47, as said below
- factor_left: bfloat16 [16, 48, 512, 512], P('rep', 'own'), may hold values from -8 to 24, as said below
- factor_right: bfloat16 [16, 48, 512, 512], P('rep', 'own'), may hold values from -8 to 24, as said below
- basis_left: bfloat16 [16, 48, 512, 512], P('rep', 'own'), may hold values from -1 to 2, as said below
- basis_right: bfloat16 [16, 48, 512, 512], P('rep', 'own'), may hold values from -1 to 2, as said below
- moment_first: bfloat16 [16, 48, 512, 512], P('rep', 'own'), may hold values from -0.125 to 0.125
- moment_second: bfloat16 [16, 48, 512, 512], P('rep', 'own'), may hold values from 0.0019989014 to 0.0079956055
Outputs:
- update: bfloat16 [48, 2, 32, 8192], P('own')
The draws below stay inside these ranges and needn't reach their ends.
Inputs may be any that keep to these rules, and one draw needn't show every extreme that they name: `owner`: within each column c the 6 entries differ, so a device owns at most one block. `factor_left`: each block is symmetric positive definite. `factor_right`: each block is symmetric positive definite. `basis_left`: each block is nonsingular and well conditioned. `basis_right`: each block is nonsingular and well conditioned.
All inputs are finite; a program needn't handle non-finite values.
Results may differ from the reference program's by a relative error of at most 0.029.
Values may be sent and summed in bfloat16 or wider, within the bound.
No kernel may reach another device: no remote copies, remote signals or barrier semaphores. Data moves between devices by JAX's collectives and lax.ppermute only.
A program may use at most 64 MiB of HBM per device.

```python
import math
import jax
import jax.numpy as jnp
from jax import lax

BLOCK = 512
ROWS_DEV = 2
SPAN = 16
SLAB = 32
GROUPS = 3
BLOCK_ROWS = 6
COLS = 8192
N_REP = 16
N_OWN = 48


def draw_owner(key, part):
    key = jax.random.fold_in(key, 11)
    column_keys = jax.random.split(key, N_REP)

    def column(one_key):
        key_pick, key_order = jax.random.split(one_key)
        middle = jax.random.permutation(key_pick, N_OWN - 2).astype(jnp.int32) + 1
        chosen = jnp.concatenate([jnp.array([0, N_OWN - 1], jnp.int32), middle[:BLOCK_ROWS - 2]])
        shuffle = jax.random.permutation(key_order, BLOCK_ROWS)
        return chosen[shuffle]
    return jax.vmap(column)(column_keys).T


def assemble_factor(scales, noise_matrix):
    root_scale = jnp.sqrt(scales)
    off_diagonal = (noise_matrix + jnp.swapaxes(noise_matrix, -1, -2)) * (0.3 / math.sqrt(2.0 * BLOCK))
    identity = jnp.eye(BLOCK, dtype=jnp.float32)
    return root_scale[..., :, None] * (identity + off_diagonal) * root_scale[..., None, :]


def draw_factor_left(key, part):
    key = jax.random.fold_in(key, 21)
    key_scale, key_noise = jax.random.split(key)
    scales = jnp.exp(jax.random.uniform(key_scale, (N_REP, N_OWN, BLOCK), minval=0.0, maxval=math.log(10.0)))
    noise_matrix = jax.random.normal(key_noise, (N_REP, N_OWN, BLOCK, BLOCK))
    return assemble_factor(scales, noise_matrix).astype(jnp.bfloat16)


def draw_factor_right(key, part):
    key = jax.random.fold_in(key, 22)
    key_scale, key_noise = jax.random.split(key)
    scales = jnp.exp(jax.random.uniform(key_scale, (N_REP, N_OWN, BLOCK), minval=0.0, maxval=math.log(10.0)))
    noise_matrix = jax.random.normal(key_noise, (N_REP, N_OWN, BLOCK, BLOCK))
    return assemble_factor(scales, noise_matrix).astype(jnp.bfloat16)


def assemble_basis(noise_matrix):
    return jnp.eye(BLOCK, dtype=jnp.float32) + noise_matrix * (0.3 / math.sqrt(1.0 * BLOCK))


def draw_basis_left(key, part):
    key = jax.random.fold_in(key, 31)
    noise_matrix = jax.random.normal(key, (N_REP, N_OWN, BLOCK, BLOCK))
    return assemble_basis(noise_matrix).astype(jnp.bfloat16)


def draw_basis_right(key, part):
    key = jax.random.fold_in(key, 32)
    noise_matrix = jax.random.normal(key, (N_REP, N_OWN, BLOCK, BLOCK))
    return assemble_basis(noise_matrix).astype(jnp.bfloat16)


def spiked(values, key, source, target, parts, factor):
    def block_of(dim):
        return (jnp.arange(values.shape[dim]) // (values.shape[dim] // parts)).reshape((-1,) + (1,) * (values.ndim - 1 - dim))

    first = jax.random.permutation(key, parts)[block_of(target)]
    far = (block_of(target) + parts // 2) % parts
    return jnp.where((block_of(source) == first) | (block_of(source) == far), factor * values, values)


def block_scale(rng, extent, cuts, low, top_value):
    level = 1.0
    for axis_at, shards_of in cuts:
        draws = jax.random.uniform(jax.random.fold_in(jax.random.fold_in(rng, 6), axis_at), (shards_of,), jnp.float32, low / len(cuts), top_value / len(cuts))
        level = level * jnp.repeat(jnp.exp(draws), extent[axis_at] // shards_of).reshape((-1,) + (1,) * (len(extent) - 1 - axis_at))
    return level


def scatter_about(key, dims, spread, bound, cuts=(), kind=jnp.bfloat16):
    loudness = block_scale(key, dims, cuts, -0.22, 0.18) if cuts else 1.0
    drawn = jax.random.normal(key, dims, jnp.float32) * spread * loudness
    return jnp.minimum(jnp.maximum(drawn, -bound), bound).astype(kind)


def gaussian_with(key, shape, scale, limit, cuts, heavy, kind=jnp.bfloat16):
    result = scale * jax.random.normal(key, shape, jnp.float32)
    if cuts:
        result = result * block_scale(key, shape, cuts, -0.22, 0.18)
    return jnp.clip(spiked(result, jax.random.fold_in(key, 3), *heavy), -limit, limit).astype(kind)


def setup_inputs(seed: int = 0) -> dict:
    keys = jax.random.split(jax.random.key(seed), 9)
    return {
        "grad_partial": gaussian_with(keys[0], (N_REP, N_OWN, ROWS_DEV, SLAB, COLS), 0.05, 0.4375, ((0, 16), (1, 48)), (0, 4, 16, 2.0)),
        "owner": draw_owner(jax.random.fold_in(keys[8], 71), 0),
        "factor_left": draw_factor_left(jax.random.fold_in(keys[8], 71), 0),
        "factor_right": draw_factor_right(jax.random.fold_in(keys[8], 71), 0),
        "basis_left": draw_basis_left(jax.random.fold_in(keys[8], 71), 0),
        "basis_right": draw_basis_right(jax.random.fold_in(keys[8], 71), 0),
        "moment_first": scatter_about(keys[6], (N_REP, N_OWN, BLOCK, BLOCK), 0.02, 0.125, ((0, 16), (1, 48))),
        "moment_second": jnp.clip(jnp.exp(math.log(0.0079956055) - 1.3862944 * jax.random.uniform(keys[7], (N_REP, N_OWN, BLOCK, BLOCK), jnp.float32) ** block_scale(keys[7], (N_REP, N_OWN, BLOCK, BLOCK), ((0, 16), (1, 48)), -0.2, 0.2)), 0.0019989014, 0.0079956055).astype(jnp.bfloat16),
    }


BETA_ONE = 0.9
BETA_TWO = 0.95
EPSILON = 1e-08

def orthonormal(matrix):
    gram_matrix = jnp.dot(matrix.T, matrix, precision=lax.Precision.HIGHEST)
    lower_factor = jnp.linalg.cholesky(gram_matrix)
    return jax.scipy.linalg.solve_triangular(lower_factor, matrix.T, lower=True).T

def soap_block(gradient, left_factor, right_factor, left_basis, right_basis, first_moment, second_moment):
    left_new = BETA_TWO * left_factor.astype(jnp.float32) + (1.0 - BETA_TWO) * jnp.dot(gradient.astype(jnp.float32), gradient.T.astype(jnp.float32), preferred_element_type=jnp.float32)
    right_new = BETA_TWO * right_factor.astype(jnp.float32) + (1.0 - BETA_TWO) * jnp.dot(gradient.T.astype(jnp.float32), gradient.astype(jnp.float32), preferred_element_type=jnp.float32)
    left_power = jnp.dot(left_new, left_basis.astype(jnp.float32), precision=lax.Precision.HIGHEST)
    right_power = jnp.dot(right_new, right_basis.astype(jnp.float32), precision=lax.Precision.HIGHEST)
    left_rotation = orthonormal(left_power).astype(jnp.bfloat16)
    right_rotation = orthonormal(right_power).astype(jnp.bfloat16)
    half_turn = jnp.dot(left_rotation.T.astype(jnp.float32), gradient.astype(jnp.float32), preferred_element_type=jnp.float32).astype(jnp.bfloat16)
    rotated = jnp.dot(half_turn.astype(jnp.float32), right_rotation.astype(jnp.float32), preferred_element_type=jnp.float32)
    first_new = BETA_ONE * first_moment.astype(jnp.float32) + (1.0 - BETA_ONE) * rotated
    second_new = BETA_TWO * second_moment.astype(jnp.float32) + (1.0 - BETA_TWO) * rotated * rotated
    direction = (first_new / (jnp.sqrt(second_new) + EPSILON)).astype(jnp.bfloat16)
    turned = jnp.dot(left_rotation.astype(jnp.float32), direction.astype(jnp.float32), preferred_element_type=jnp.float32).astype(jnp.bfloat16)
    return jnp.dot(turned.astype(jnp.float32), right_rotation.T.astype(jnp.float32), preferred_element_type=jnp.float32).astype(jnp.bfloat16)

def reference(grad_partial, owner, factor_left, factor_right, basis_left, basis_right, moment_first, moment_second):
    grad = lax.optimization_barrier(jnp.sum(grad_partial.astype(jnp.float32), axis=0)).astype(jnp.bfloat16)
    blocks = grad.reshape(GROUPS, SPAN, ROWS_DEV, SLAB, N_REP, BLOCK)
    blocks = blocks.transpose(0, 2, 4, 1, 3, 5).reshape(BLOCK_ROWS * N_REP, BLOCK, BLOCK)
    slot_index = (jnp.arange(N_REP, dtype=jnp.int32)[None, :] * N_OWN + owner.astype(jnp.int32)).reshape(-1)
    states = tuple((item.reshape(N_REP * N_OWN, BLOCK, BLOCK) for item in (factor_left, factor_right, basis_left, basis_right, moment_first, moment_second)))

    def process(entry):
        gradient, slot = entry
        return soap_block(gradient, states[0][slot], states[1][slot], states[2][slot], states[3][slot], states[4][slot], states[5][slot])
    updates = lax.map(process, (blocks, slot_index))
    updates = updates.reshape(GROUPS, ROWS_DEV, N_REP, SPAN, SLAB, BLOCK)
    return updates.transpose(0, 3, 1, 4, 2, 5).reshape(N_OWN, ROWS_DEV, SLAB, COLS)
```

```python
import jax
import jax.numpy as jnp
import numpy as np
from jax import lax
from jax.experimental import pallas as pl
from jax.experimental.pallas import tpu as pltpu
from jax.sharding import Mesh
from jax.sharding import PartitionSpec as P

BETA_ONE = 0.9
BETA_TWO = 0.95
EPSILON = 1e-08
PANEL = 128
GROUP = 8
F32 = jnp.float32
BF16 = jnp.bfloat16
NN = (((1,), (0,)), ((), ()))
NT = (((1,), (1,)), ((), ()))
TN = (((0,), (0,)), ((), ()))


def dot(a, b, dims, precision=None):
    return lax.dot_general(a, b, dims, precision=precision, preferred_element_type=F32)


def exact(a, b, dims):
    return dot(a, b, dims, lax.Precision.HIGHEST)


def times_bf16(a, b):
    high = a.astype(BF16)
    rest = a - high.astype(F32)
    middle = rest.astype(BF16)
    low = (rest - middle.astype(F32)).astype(BF16)
    return dot(low, b, NN) + dot(middle, b, NN) + dot(high, b, NN)


def inverse_factors(grams):
    rows = PANEL // GROUP
    lane = lax.broadcasted_iota(jnp.int32, (GROUP, PANEL), 1)
    sub = lax.broadcasted_iota(jnp.int32, (GROUP, PANEL), 0)
    tiles = [[g[GROUP * r : GROUP * (r + 1), :] for r in range(rows)] for g in grams]
    for p in range(rows):
        first = GROUP * p
        columns = [
            [
                [jnp.broadcast_to(t[r][:, first + j : first + j + 1], (GROUP, PANEL)) for r in range(p, rows)]
                for j in range(GROUP)
            ]
            for t in tiles
        ]
        in_group = (lane >= first) & (lane < first + GROUP)
        for t in tiles:
            for r in range(p + 1, rows):
                t[r] = jnp.where(in_group, 0.0, t[r])
        for j in range(GROUP):
            for t, c in zip(tiles, columns):
                pivot = jnp.broadcast_to(c[j][0][j : j + 1, :], (GROUP, PANEL))
                scale = lax.rsqrt(pivot)
                top = jnp.broadcast_to(t[p][j : j + 1, :], (GROUP, PANEL))
                row = jnp.where(lane == first + j, scale, top * scale)
                multipliers = [x * scale for x in c[j]]
                multipliers[0] = jnp.where(sub > j, multipliers[0], 0.0)
                below = jnp.where(lane == first + j, 0.0, t[p]) - multipliers[0] * row
                t[p] = jnp.where(sub == j, row, jnp.where(sub > j, below, t[p]))
                row = jnp.where((lane > first + j) & (lane < first + GROUP), 0.0, row)
                for r in range(p + 1, rows):
                    t[r] = t[r] - multipliers[r - p] * row
                for k in range(j + 1, GROUP):
                    factor = jnp.broadcast_to(multipliers[0][k : k + 1, :], (GROUP, PANEL))
                    c[k] = [x - m * factor for x, m in zip(c[k], multipliers)]
    row_of = [sub + GROUP * r for r in range(rows)]
    return [
        jnp.concatenate([jnp.where(lane <= i, x, 0.0) for i, x in zip(row_of, t)], axis=0)
        for t in tiles
    ]


def block_kernel(g_ref, fl_ref, fr_ref, bl_ref, br_ref, m1_ref, m2_ref, out_ref, ml, mr, ql, qr):
    size = g_ref.shape[0]
    gradient = g_ref[...]
    left = BETA_TWO * fl_ref[...].astype(F32) + (1.0 - BETA_TWO) * dot(gradient, gradient, NT)
    right = BETA_TWO * fr_ref[...].astype(F32) + (1.0 - BETA_TWO) * dot(gradient, gradient, TN)
    ml[...] = times_bf16(left, bl_ref[...])
    mr[...] = times_bf16(right, br_ref[...])
    def step(index, carry):
        here = pl.ds(pl.multiple_of(index * PANEL, PANEL), PANEL)
        grams = []
        for m in (ml, mr):
            panel = m[:, here]
            grams.append(exact(panel, panel, TN))
        inverses = inverse_factors(grams)
        for m, q, inverse in zip((ml, mr), (ql, qr), inverses):
            basis = exact(m[:, here], inverse, NT)
            q[:, here] = basis.astype(BF16)
            m[:, here] = basis
        for done in range(size // PANEL - 1):

            @pl.when(index == done)
            def _():
                rest = slice((done + 1) * PANEL, size)
                for m in (ml, mr):
                    basis = m[:, done * PANEL : (done + 1) * PANEL]
                    m[:, rest] = m[:, rest] - exact(basis, exact(basis, m[:, rest], TN), NN)

        return carry

    lax.fori_loop(0, size // PANEL, step, 0)
    left_rotation = ql[...]
    right_rotation = qr[...]
    half = dot(left_rotation, gradient, TN).astype(BF16)
    rotated = dot(half, right_rotation, NN)
    first_new = BETA_ONE * m1_ref[...].astype(F32) + (1.0 - BETA_ONE) * rotated
    second_new = BETA_TWO * m2_ref[...].astype(F32) + (1.0 - BETA_TWO) * rotated * rotated
    direction = (first_new / (jnp.sqrt(second_new) + EPSILON)).astype(BF16)
    turned = dot(left_rotation, direction, NN).astype(BF16)
    out_ref[...] = dot(turned, right_rotation, NT).astype(BF16)


def soap_block(*operands):
    size = operands[0].shape[0]
    return pl.pallas_call(
        block_kernel,
        out_shape=jax.ShapeDtypeStruct((size, size), BF16),
        in_specs=[pl.BlockSpec(memory_space=pltpu.VMEM)] * len(operands),
        out_specs=pl.BlockSpec(memory_space=pltpu.VMEM),
        scratch_shapes=[pltpu.VMEM((size, size), F32)] * 2 + [pltpu.VMEM((size, size), BF16)] * 2,
        compiler_params=pltpu.CompilerParams(vmem_limit_bytes=32 * 1024 * 1024),
        name="soap_block",
    )(*operands)


def reduce_columns(grad):
    ring, cores = lax.axis_size("y"), lax.axis_size("core")
    rows, columns = grad.shape
    blocks = grad.reshape(rows, ring, cores, columns // (ring * cores))
    even = blocks[:, :, 0].transpose(1, 0, 2)
    odd = blocks[:, :, 1].transpose(1, 0, 2)
    first_core = lax.axis_index("core") == 0
    sent = jnp.where(first_core, odd, even)
    kept = jnp.where(first_core, even, odd)
    received = lax.ppermute(sent, "core", [(0, 1), (1, 0)])
    pair_sum = (kept.astype(F32) + received.astype(F32)).astype(BF16)
    parts = lax.all_to_all(pair_sum, "y", 0, 0, tiled=True)
    return jnp.sum(parts.astype(F32), axis=0).astype(BF16)


def gather_columns(piece):
    ring = lax.axis_size("y")
    rows, width = piece.shape
    spread = jnp.broadcast_to(piece[None], (ring, rows, width))
    mine = lax.all_to_all(spread, "y", 0, 0, tiled=True)
    other = lax.ppermute(mine, "core", [(0, 1), (1, 0)])
    first_core = lax.axis_index("core") == 0
    even = jnp.where(first_core, mine, other)
    odd = jnp.where(first_core, other, mine)
    both = jnp.stack([even, odd], axis=1)
    return both.transpose(2, 0, 1, 3).reshape(rows, -1)


def per_device(
    grad_partial,
    owner,
    factor_left,
    factor_right,
    basis_left,
    basis_right,
    moment_first,
    moment_second,
):
    own_count = lax.axis_size(("x", "z"))
    position = lax.axis_index(("x", "z"))
    column = lax.axis_index(("y", "core"))
    rows_here, slab_rows, width = grad_partial.shape[2:]
    block = factor_left.shape[-1]
    group_span = block // slab_rows
    owners_here = lax.dynamic_slice_in_dim(owner, column, 1, 1)[:, 0]
    targets = lax.dynamic_slice_in_dim(
        owners_here, position // group_span * rows_here, rows_here, 0
    )
    owned_row = jnp.sum(
        jnp.where(owners_here == position, jnp.arange(owners_here.shape[0], dtype=jnp.int32), 0)
    )
    owned_group = owned_row // rows_here
    summed = reduce_columns(grad_partial.reshape(rows_here * slab_rows, width))
    summed = summed.reshape(rows_here, slab_rows, block)
    slots = jnp.arange(own_count, dtype=jnp.int32)[:, None, None]
    outgoing = jnp.where(slots == targets[1], summed[1][None], summed[0][None])
    arrived = lax.all_to_all(outgoing, ("x", "z"), 0, 0, tiled=True)
    gradient = lax.dynamic_slice_in_dim(arrived, owned_group * group_span, group_span, 0)
    update = soap_block(
        gradient.reshape(block, block),
        factor_left[0, 0],
        factor_right[0, 0],
        basis_left[0, 0],
        basis_right[0, 0],
        moment_first[0, 0],
        moment_second[0, 0],
    )
    pieces = update.reshape(group_span, slab_rows, block)
    outgoing_back = jnp.concatenate([pieces] * (own_count // group_span), axis=0)
    returned = lax.all_to_all(outgoing_back, ("x", "z"), 0, 0, tiled=True)
    own_update = jnp.concatenate(
        [lax.dynamic_index_in_dim(returned, targets[r], 0, keepdims=False) for r in range(rows_here)]
    )
    return gather_columns(own_update).reshape(1, rows_here, slab_rows, width)


def solution(mesh):
    chips = Mesh(mesh.devices.reshape(8, 2, 4, 12), ("y", "core", "x", "z"))
    rep, own = ("y", "core"), ("x", "z")
    state = P(rep, own, None, None)
    return jax.shard_map(
        per_device,
        mesh=chips,
        in_specs=(P(rep, own, None, None, None), P()) + (state,) * 6,
        out_specs=P(own, None, None, None),
        check_vma=False,
    )
```

```python
import jax
import jax.numpy as jnp
from jax import lax
from jax.experimental import pallas as pl
from jax.experimental.pallas import tpu as pltpu
from jax.sharding import Mesh
from jax.sharding import PartitionSpec as P

BETA_ONE = 0.9
BETA_TWO = 0.95
EPSILON = 1e-08
PANEL = 128
GROUP = 8
F32 = jnp.float32
BF16 = jnp.bfloat16
NN = (((1,), (0,)), ((), ()))
NT = (((1,), (1,)), ((), ()))
TN = (((0,), (0,)), ((), ()))


def dot(a, b, dims, precision=None):
    return lax.dot_general(a, b, dims, precision=precision, preferred_element_type=F32)


def exact(a, b, dims):
    return dot(a, b, dims, lax.Precision.HIGHEST)


def times_bf16(a, b):
    high = a.astype(BF16)
    rest = a - high.astype(F32)
    middle = rest.astype(BF16)
    low = (rest - middle.astype(F32)).astype(BF16)
    return dot(low, b, NN) + dot(middle, b, NN) + dot(high, b, NN)


def inverse_factors(grams):
    rows = PANEL // GROUP
    lane = lax.broadcasted_iota(jnp.int32, (GROUP, PANEL), 1)
    sub = lax.broadcasted_iota(jnp.int32, (GROUP, PANEL), 0)
    tiles = [[g[GROUP * r : GROUP * (r + 1), :] for r in range(rows)] for g in grams]
    for p in range(rows):
        first = GROUP * p
        columns = [
            [
                [jnp.broadcast_to(t[r][:, first + j : first + j + 1], (GROUP, PANEL)) for r in range(p, rows)]
                for j in range(GROUP)
            ]
            for t in tiles
        ]
        in_group = (lane >= first) & (lane < first + GROUP)
        for t in tiles:
            for r in range(p + 1, rows):
                t[r] = jnp.where(in_group, 0.0, t[r])
        for j in range(GROUP):
            for t, c in zip(tiles, columns):
                pivot = jnp.broadcast_to(c[j][0][j : j + 1, :], (GROUP, PANEL))
                scale = lax.rsqrt(pivot)
                top = jnp.broadcast_to(t[p][j : j + 1, :], (GROUP, PANEL))
                row = jnp.where(lane == first + j, scale, top * scale)
                multipliers = [x * scale for x in c[j]]
                multipliers[0] = jnp.where(sub > j, multipliers[0], 0.0)
                below = jnp.where(lane == first + j, 0.0, t[p]) - multipliers[0] * row
                t[p] = jnp.where(sub == j, row, jnp.where(sub > j, below, t[p]))
                row = jnp.where((lane > first + j) & (lane < first + GROUP), 0.0, row)
                for r in range(p + 1, rows):
                    t[r] = t[r] - multipliers[r - p] * row
                for k in range(j + 1, GROUP):
                    factor = jnp.broadcast_to(multipliers[0][k : k + 1, :], (GROUP, PANEL))
                    c[k] = [x - m * factor for x, m in zip(c[k], multipliers)]
    row_of = [sub + GROUP * r for r in range(rows)]
    return [
        jnp.concatenate([jnp.where(lane <= i, x, 0.0) for i, x in zip(row_of, t)], axis=0)
        for t in tiles
    ]


def block_kernel(
    order, slots, arrived, fl_ref, fr_ref, bl_ref, br_ref, m1_ref, m2_ref, out_ref, ml, mr, ql, qr, rows_ref
):
    size = fl_ref.shape[0]
    slab = arrived.shape[1]
    for i in range(size // slab):
        rows_ref[i] = arrived[order[i]]
    gradient = rows_ref[...].reshape(size, size)
    left = BETA_TWO * fl_ref[...].astype(F32) + (1.0 - BETA_TWO) * dot(gradient, gradient, NT)
    right = BETA_TWO * fr_ref[...].astype(F32) + (1.0 - BETA_TWO) * dot(gradient, gradient, TN)
    ml[...] = times_bf16(left, bl_ref[...])
    mr[...] = times_bf16(right, br_ref[...])
    def step(index, carry):
        here = pl.ds(pl.multiple_of(index * PANEL, PANEL), PANEL)
        grams = []
        for m in (ml, mr):
            panel = m[:, here]
            grams.append(exact(panel, panel, TN))
        inverses = inverse_factors(grams)
        for m, q, inverse in zip((ml, mr), (ql, qr), inverses):
            basis = exact(m[:, here], inverse, NT)
            q[:, here] = basis.astype(BF16)
            m[:, here] = basis
        for done in range(size // PANEL - 1):

            @pl.when(index == done)
            def _():
                rest = slice((done + 1) * PANEL, size)
                for m in (ml, mr):
                    basis = m[:, done * PANEL : (done + 1) * PANEL]
                    m[:, rest] = m[:, rest] - exact(basis, exact(basis, m[:, rest], TN), NN)

        return carry

    lax.fori_loop(0, size // PANEL, step, 0)
    left_rotation = ql[...]
    right_rotation = qr[...]
    half = dot(left_rotation, gradient, TN).astype(BF16)
    rotated = dot(half, right_rotation, NN)
    first_new = BETA_ONE * m1_ref[...].astype(F32) + (1.0 - BETA_ONE) * rotated
    second_new = BETA_TWO * m2_ref[...].astype(F32) + (1.0 - BETA_TWO) * rotated * rotated
    direction = (first_new / (jnp.sqrt(second_new) + EPSILON)).astype(BF16)
    turned = dot(left_rotation, direction, NN).astype(BF16)
    rows_ref[...] = dot(turned, right_rotation, NT).astype(BF16).reshape(rows_ref.shape)
    for i in range(out_ref.shape[0]):
        out_ref[i] = rows_ref[slots[i]]


VMEM = pl.BlockSpec(memory_space=pltpu.VMEM)
SMEM = pl.BlockSpec(memory_space=pltpu.SMEM)


def soap_block(order, slots, arrived, *state):
    size = state[0].shape[0]
    slab = arrived.shape[1]
    return pl.pallas_call(
        block_kernel,
        out_shape=jax.ShapeDtypeStruct((slots.shape[0], slab, size), BF16),
        in_specs=[SMEM] * 2 + [VMEM] * (1 + len(state)),
        out_specs=VMEM,
        scratch_shapes=[pltpu.VMEM((size, size), F32)] * 2
        + [pltpu.VMEM((size, size), BF16)] * 2
        + [pltpu.VMEM((size // slab, slab, size), BF16)],
        compiler_params=pltpu.CompilerParams(vmem_limit_bytes=32 * 1024 * 1024),
        name="soap_block",
    )(order, slots, arrived, *state)


def pick_kernel(index, source, out):
    for i in range(out.shape[0]):
        out[i] = source[index[i]]


def pick(index, source):
    return pl.pallas_call(
        pick_kernel,
        out_shape=jax.ShapeDtypeStruct(index.shape + source.shape[1:], BF16),
        in_specs=[SMEM, VMEM],
        out_specs=VMEM,
        name="pick",
    )(index, source)


def split_kernel(core, grad, sent, kept):
    slabs, slab, _ = grad.shape
    ring, _, block = sent.shape
    for y in range(ring):
        mine = pl.ds(pl.multiple_of((2 * y + core[0]) * block, block), block)
        other = pl.ds(pl.multiple_of((2 * y + 1 - core[0]) * block, block), block)
        for r in range(slabs):
            rows = slice(r * slab, (r + 1) * slab)
            kept[y, rows, :] = grad[r, :, mine]
            sent[y, rows, :] = grad[r, :, other]


def join_kernel(core, mine_ref, other_ref, out):
    _, slabs, slab, _ = out.shape
    ring, _, block = mine_ref.shape
    for y in range(ring):
        mine = pl.ds(pl.multiple_of((2 * y + core[0]) * block, block), block)
        other = pl.ds(pl.multiple_of((2 * y + 1 - core[0]) * block, block), block)
        for r in range(slabs):
            rows = slice(r * slab, (r + 1) * slab)
            out[0, r, :, mine] = mine_ref[y, rows, :]
            out[0, r, :, other] = other_ref[y, rows, :]


def sum_kernel(parts, out):
    total = parts[0].astype(F32)
    for y in range(1, parts.shape[0]):
        total = total + parts[y].astype(F32)
    total = total.astype(BF16)
    for x in range(out.shape[0]):
        out[x] = total


def across(core):
    return [(i, 1 - i) for i in range(core)]


def reduce_columns(core, grad, block, copies):
    ring = lax.axis_size("y")
    rows = grad.shape[0] * grad.shape[1]
    split = jax.ShapeDtypeStruct((ring, rows, block), BF16)
    sent, kept = pl.pallas_call(
        split_kernel,
        out_shape=(split, split),
        in_specs=[SMEM, VMEM],
        out_specs=(VMEM, VMEM),
        name="split",
    )(core, grad)
    received = lax.ppermute(sent, "core", across(2))
    pair_sum = (kept.astype(F32) + received.astype(F32)).astype(BF16)
    parts = lax.all_to_all(pair_sum, "y", 0, 0, tiled=True)
    return pl.pallas_call(
        sum_kernel,
        out_shape=jax.ShapeDtypeStruct((copies, rows, block), BF16),
        in_specs=[VMEM],
        out_specs=VMEM,
        name="sum",
    )(parts)


def gather_columns(core, spread, shape):
    mine = lax.all_to_all(spread, "y", 0, 0, tiled=True)
    other = lax.ppermute(mine, "core", across(2))
    return pl.pallas_call(
        join_kernel,
        out_shape=jax.ShapeDtypeStruct(shape, BF16),
        in_specs=[SMEM, VMEM, VMEM],
        out_specs=VMEM,
        name="join",
    )(core, mine, other)


def per_device(
    grad_partial,
    owner,
    factor_left,
    factor_right,
    basis_left,
    basis_right,
    moment_first,
    moment_second,
):
    lines, ring, turn = lax.axis_size("x"), lax.axis_size("z"), lax.axis_size("y")
    here_x, here_z = lax.axis_index("x"), lax.axis_index("z")
    core = lax.axis_index("core")
    column = lax.axis_index(("y", "core"))
    slabs, slab, width = grad_partial.shape[2:]
    block = factor_left.shape[-1]
    span = block // slab
    pieces = -(-span // ring)
    owners = lax.dynamic_slice_in_dim(owner, column, 1, 1)[:, 0]
    count = owners.shape[0]

    def block_of(place):
        mine = owners[None, :] == place[:, None]
        return jnp.sum(jnp.where(mine, jnp.arange(count, dtype=jnp.int32)[None, :], 0), axis=1)

    def owner_of(row):
        match = row[:, None] == jnp.arange(count, dtype=jnp.int32)[None, :]
        return jnp.sum(jnp.where(match, owners[None, :], 0), axis=1)

    slot = jnp.arange(ring * pieces, dtype=jnp.int32)
    slot_z, slot_b = slot // pieces, slot % pieces
    wanted = block_of(here_x * ring + slot_z)
    start = wanted // slabs * span
    rows_from = start + lax.rem(here_z - lax.rem(start, ring) + ring, ring) + ring * slot_b
    send_index = jnp.minimum(rows_from // ring, lines - 1) * slabs + wanted % slabs
    owned = block_of((here_x * ring + here_z)[None])[0]
    owned_start = owned // slabs * span
    slab_number = jnp.arange(span, dtype=jnp.int32)
    order = lax.rem(owned_start + slab_number, ring) * pieces + slab_number // ring
    leave = lax.rem(slot_z - lax.rem(owned_start, ring) + ring, ring) + ring * slot_b
    leave = jnp.minimum(leave, span - 1)
    line = jnp.arange(lines * slabs, dtype=jnp.int32)
    place = line // slabs * ring + here_z
    source = owner_of(place // span * slabs + line % slabs)
    turn_index = lax.rem(source, ring) * pieces + lax.rem(place, span) // ring
    copy = jnp.arange(turn * slabs, dtype=jnp.int32) % slabs
    here = here_x * ring + here_z
    keep_index = owner_of(here // span * slabs + copy) // ring * slabs + copy

    core = core[None].astype(jnp.int32)
    summed = reduce_columns(core, grad_partial[0, 0], block, lines)
    lined = lax.all_to_all(summed, "x", 0, 0, tiled=True).reshape(lines * slabs, slab, block)
    outgoing = pick(send_index, lined).reshape(ring, pieces * slab, block)
    arrived = lax.all_to_all(outgoing, "z", 0, 0, tiled=True).reshape(ring * pieces, slab, block)
    leaving = soap_block(
        order,
        leave,
        arrived,
        factor_left[0, 0],
        factor_right[0, 0],
        basis_left[0, 0],
        basis_right[0, 0],
        moment_first[0, 0],
        moment_second[0, 0],
    ).reshape(ring, pieces * slab, block)
    back = lax.all_to_all(leaving, "z", 0, 0, tiled=True).reshape(ring * pieces, slab, block)
    turning = pick(turn_index, back).reshape(lines, slabs * slab, block)
    returned = lax.all_to_all(turning, "x", 0, 0, tiled=True).reshape(lines * slabs, slab, block)
    spread = pick(keep_index, returned).reshape(turn, slabs * slab, block)
    return gather_columns(core, spread, (1, slabs, slab, width))


def solution(mesh):
    chips = Mesh(mesh.devices.reshape(8, 2, 4, 12), ("y", "core", "x", "z"))
    rep, own = ("y", "core"), ("x", "z")
    state = P(rep, own, None, None)
    return jax.shard_map(
        per_device,
        mesh=chips,
        in_specs=(P(rep, own, None, None, None), P()) + (state,) * 6,
        out_specs=P(own, None, None, None),
        check_vma=False,
    )
```

```python
import jax
import jax.numpy as jnp
from jax import lax
from jax.experimental import pallas as pl
from jax.experimental.pallas import tpu as pltpu
from jax.sharding import Mesh
from jax.sharding import PartitionSpec as P

BETA_ONE = 0.9
BETA_TWO = 0.95
EPSILON = 1e-08
PANEL = 128
GROUP = 8
F32 = jnp.float32
BF16 = jnp.bfloat16
NN = (((1,), (0,)), ((), ()))
NT = (((1,), (1,)), ((), ()))
TN = (((0,), (0,)), ((), ()))


def dot(a, b, dims, precision=None):
    return lax.dot_general(a, b, dims, precision=precision, preferred_element_type=F32)


def exact(a, b, dims):
    return dot(a, b, dims, lax.Precision.HIGHEST)


def times_bf16(a, b):
    high = a.astype(BF16)
    rest = a - high.astype(F32)
    middle = rest.astype(BF16)
    low = (rest - middle.astype(F32)).astype(BF16)
    return dot(low, b, NN) + dot(middle, b, NN) + dot(high, b, NN)


def three_terms(x):
    high = x.astype(BF16).astype(F32)
    middle = (x - high).astype(BF16).astype(F32)
    return high, middle, (x - high) - middle


def inverse_factors(grams):
    rows = PANEL // GROUP
    tile = (GROUP, PANEL)
    lane = lax.broadcasted_iota(jnp.int32, tile, 1)
    sub = lax.broadcasted_iota(jnp.int32, tile, 0)
    tiles = [[g[GROUP * r : GROUP * (r + 1), :] for r in range(rows)] for g in grams]
    for p in range(rows):
        first = GROUP * p
        in_group = (lane >= first) & (lane < first + GROUP)
        unit = jnp.where(lane == first + sub, 1.0, 0.0)
        for t in tiles:
            columns = [
                [jnp.broadcast_to(t[r][:, first + j : first + j + 1], tile) for r in range(p, min(p + 2, rows))]
                for j in range(GROUP)
            ]
            square = [
                [jnp.broadcast_to(columns[j][0][i : i + 1, :], tile) if i >= j else None for j in range(GROUP)]
                for i in range(GROUP)
            ]
            scales = []
            for j in range(GROUP):
                scale = lax.rsqrt(square[j][j])
                scales.append(scale)
                for i in range(j + 1, GROUP):
                    square[i][j] = square[i][j] * scale
                for k in range(j + 1, GROUP):
                    for i in range(k, GROUP):
                        square[i][k] = square[i][k] - square[i][j] * square[k][j]
            top = jnp.where(in_group, unit, t[p])
            solved = [jnp.broadcast_to(top[j : j + 1, :], tile) for j in range(GROUP)]
            for j in range(GROUP):
                solved[j] = solved[j] * scales[j]
                for i in range(j + 1, GROUP):
                    solved[i] = solved[i] - square[i][j] * solved[j]
            done = solved[0]
            for j in range(1, GROUP):
                done = jnp.where(sub == j, solved[j], done)
            t[p] = done
            if p + 1 < rows:
                below = [c[1] for c in columns]
                rest = jnp.where(in_group, 0.0, t[p + 1])
                for j in range(GROUP):
                    below[j] = below[j] * scales[j]
                    for i in range(j + 1, GROUP):
                        below[i] = below[i] - square[i][j] * below[j]
                    rest = rest - below[j] * solved[j]
                t[p + 1] = rest
            if p + 2 < rows:
                high, middle, low = three_terms(done)
                left = [jnp.where(lane >= first + 2 * GROUP, x, 0.0) for x in (high, middle, low)]
                lhs = jnp.concatenate([left[i] for i in (0, 1, 0, 2, 0, 1)], axis=0)
                rhs = jnp.concatenate([high, high, middle, high, low, middle], axis=0)
                product = dot(lhs.astype(BF16), rhs.astype(BF16), TN)
                for r in range(p + 2, rows):
                    rest = jnp.where(in_group, 0.0, t[r])
                    t[r] = rest - product[GROUP * r : GROUP * (r + 1), :]
    return [
        jnp.concatenate(
            [jnp.where(lane <= sub + GROUP * r, x, 0.0) for r, x in enumerate(t)], axis=0
        )
        for t in tiles
    ]


def block_kernel(
    order, slots, arrived, fl_ref, fr_ref, bl_ref, br_ref, m1_ref, m2_ref, out_ref, ml, mr, ql, qr, rows_ref
):
    size = fl_ref.shape[0]
    slab = arrived.shape[1]
    for i in range(size // slab):
        rows_ref[i] = arrived[order[i]]
    gradient = rows_ref[...].reshape(size, size)
    left = BETA_TWO * fl_ref[...].astype(F32) + (1.0 - BETA_TWO) * dot(gradient, gradient, NT)
    right = BETA_TWO * fr_ref[...].astype(F32) + (1.0 - BETA_TWO) * dot(gradient, gradient, TN)
    ml[...] = times_bf16(left, bl_ref[...])
    mr[...] = times_bf16(right, br_ref[...])
    def step(index, carry):
        here = pl.ds(pl.multiple_of(index * PANEL, PANEL), PANEL)
        grams = []
        for m in (ml, mr):
            panel = m[:, here]
            grams.append(exact(panel, panel, TN))
        inverses = inverse_factors(grams)
        for m, q, inverse in zip((ml, mr), (ql, qr), inverses):
            basis = exact(m[:, here], inverse, NT)
            q[:, here] = basis.astype(BF16)
            m[:, here] = basis
        for done in range(size // PANEL - 1):

            @pl.when(index == done)
            def _():
                rest = slice((done + 1) * PANEL, size)
                for m in (ml, mr):
                    basis = m[:, done * PANEL : (done + 1) * PANEL]
                    m[:, rest] = m[:, rest] - exact(basis, exact(basis, m[:, rest], TN), NN)

        return carry

    lax.fori_loop(0, size // PANEL, step, 0)
    left_rotation = ql[...]
    right_rotation = qr[...]
    half = dot(left_rotation, gradient, TN).astype(BF16)
    rotated = dot(half, right_rotation, NN)
    first_new = BETA_ONE * m1_ref[...].astype(F32) + (1.0 - BETA_ONE) * rotated
    second_new = BETA_TWO * m2_ref[...].astype(F32) + (1.0 - BETA_TWO) * rotated * rotated
    direction = (first_new / (jnp.sqrt(second_new) + EPSILON)).astype(BF16)
    turned = dot(left_rotation, direction, NN).astype(BF16)
    rows_ref[...] = dot(turned, right_rotation, NT).astype(BF16).reshape(rows_ref.shape)
    for i in range(out_ref.shape[0]):
        out_ref[i] = rows_ref[slots[i]]


VMEM = pl.BlockSpec(memory_space=pltpu.VMEM)
SMEM = pl.BlockSpec(memory_space=pltpu.SMEM)
SMALL = pltpu.CompilerParams(vmem_limit_bytes=8 * 1024 * 1024)


def soap_block(order, slots, arrived, *state):
    size = state[0].shape[0]
    slab = arrived.shape[1]
    return pl.pallas_call(
        block_kernel,
        out_shape=jax.ShapeDtypeStruct((slots.shape[0], slab, size), BF16),
        in_specs=[SMEM] * 2 + [VMEM] * (1 + len(state)),
        out_specs=VMEM,
        scratch_shapes=[pltpu.VMEM((size, size), F32)] * 2
        + [pltpu.VMEM((size, size), BF16)] * 2
        + [pltpu.VMEM((size // slab, slab, size), BF16)],
        compiler_params=pltpu.CompilerParams(vmem_limit_bytes=32 * 1024 * 1024),
        name="soap_block",
    )(order, slots, arrived, *state)


def pick_kernel(index, source, out):
    for i in range(out.shape[0]):
        out[i] = source[index[i]]


def pick(index, source):
    return pl.pallas_call(
        pick_kernel,
        out_shape=jax.ShapeDtypeStruct(index.shape + source.shape[1:], BF16),
        in_specs=[SMEM, VMEM],
        out_specs=VMEM,
        compiler_params=SMALL,
        name="pick",
    )(index, source)


def split_kernel(core, grad, sent, kept):
    slabs, slab, _ = grad.shape
    ring, _, block = sent.shape
    for y in range(ring):
        mine = pl.ds(pl.multiple_of((2 * y + core[0]) * block, block), block)
        other = pl.ds(pl.multiple_of((2 * y + 1 - core[0]) * block, block), block)
        for r in range(slabs):
            rows = slice(r * slab, (r + 1) * slab)
            kept[y, rows, :] = grad[r, :, mine]
            sent[y, rows, :] = grad[r, :, other]


def join_kernel(core, mine_ref, other_ref, out):
    _, slabs, slab, _ = out.shape
    ring, _, block = mine_ref.shape
    for y in range(ring):
        mine = pl.ds(pl.multiple_of((2 * y + core[0]) * block, block), block)
        other = pl.ds(pl.multiple_of((2 * y + 1 - core[0]) * block, block), block)
        for r in range(slabs):
            rows = slice(r * slab, (r + 1) * slab)
            out[0, r, :, mine] = mine_ref[y, rows, :]
            out[0, r, :, other] = other_ref[y, rows, :]


def sum_kernel(parts, out):
    total = parts[0].astype(F32)
    for y in range(1, parts.shape[0]):
        total = total + parts[y].astype(F32)
    total = total.astype(BF16)
    for x in range(out.shape[0]):
        out[x] = total


def across(core):
    return [(i, 1 - i) for i in range(core)]


def reduce_columns(core, grad, block, copies):
    ring = lax.axis_size("y")
    rows = grad.shape[0] * grad.shape[1]
    split = jax.ShapeDtypeStruct((ring, rows, block), BF16)
    sent, kept = pl.pallas_call(
        split_kernel,
        out_shape=(split, split),
        in_specs=[SMEM, VMEM],
        out_specs=(VMEM, VMEM),
        compiler_params=SMALL,
        name="split",
    )(core, grad)
    received = lax.ppermute(sent, "core", across(2))
    pair_sum = (kept.astype(F32) + received.astype(F32)).astype(BF16)
    parts = lax.all_to_all(pair_sum, "y", 0, 0, tiled=True)
    return pl.pallas_call(
        sum_kernel,
        out_shape=jax.ShapeDtypeStruct((copies, rows, block), BF16),
        in_specs=[VMEM],
        out_specs=VMEM,
        compiler_params=SMALL,
        name="sum",
    )(parts)


def gather_columns(core, spread, shape):
    mine = lax.all_to_all(spread, "y", 0, 0, tiled=True)
    other = lax.ppermute(mine, "core", across(2))
    return pl.pallas_call(
        join_kernel,
        out_shape=jax.ShapeDtypeStruct(shape, BF16),
        in_specs=[SMEM, VMEM, VMEM],
        out_specs=VMEM,
        compiler_params=SMALL,
        name="join",
    )(core, mine, other)


def per_device(
    grad_partial,
    owner,
    factor_left,
    factor_right,
    basis_left,
    basis_right,
    moment_first,
    moment_second,
):
    lines, ring, turn = lax.axis_size("x"), lax.axis_size("z"), lax.axis_size("y")
    here_x, here_z = lax.axis_index("x"), lax.axis_index("z")
    core = lax.axis_index("core")
    column = lax.axis_index(("y", "core"))
    slabs, slab, width = grad_partial.shape[2:]
    block = factor_left.shape[-1]
    span = block // slab
    pieces = -(-span // ring)
    owners = lax.dynamic_slice_in_dim(owner, column, 1, 1)[:, 0]
    count = owners.shape[0]

    def block_of(place):
        mine = owners[None, :] == place[:, None]
        return jnp.sum(jnp.where(mine, jnp.arange(count, dtype=jnp.int32)[None, :], 0), axis=1)

    def owner_of(row):
        match = row[:, None] == jnp.arange(count, dtype=jnp.int32)[None, :]
        return jnp.sum(jnp.where(match, owners[None, :], 0), axis=1)

    slot = jnp.arange(ring * pieces, dtype=jnp.int32)
    slot_z, slot_b = slot // pieces, slot % pieces
    wanted = block_of(here_x * ring + slot_z)
    start = wanted // slabs * span
    rows_from = start + lax.rem(here_z - lax.rem(start, ring) + ring, ring) + ring * slot_b
    send_index = jnp.minimum(rows_from // ring, lines - 1) * slabs + wanted % slabs
    owned = block_of((here_x * ring + here_z)[None])[0]
    owned_start = owned // slabs * span
    slab_number = jnp.arange(span, dtype=jnp.int32)
    order = lax.rem(owned_start + slab_number, ring) * pieces + slab_number // ring
    leave = lax.rem(slot_z - lax.rem(owned_start, ring) + ring, ring) + ring * slot_b
    leave = jnp.minimum(leave, span - 1)
    line = jnp.arange(lines * slabs, dtype=jnp.int32)
    place = line // slabs * ring + here_z
    source = owner_of(place // span * slabs + line % slabs)
    turn_index = lax.rem(source, ring) * pieces + lax.rem(place, span) // ring
    copy = jnp.arange(turn * slabs, dtype=jnp.int32) % slabs
    here = here_x * ring + here_z
    keep_index = owner_of(here // span * slabs + copy) // ring * slabs + copy

    core = core[None].astype(jnp.int32)
    summed = reduce_columns(core, grad_partial[0, 0], block, lines)
    lined = lax.all_to_all(summed, "x", 0, 0, tiled=True).reshape(lines * slabs, slab, block)
    outgoing = pick(send_index, lined).reshape(ring, pieces * slab, block)
    arrived = lax.all_to_all(outgoing, "z", 0, 0, tiled=True).reshape(ring * pieces, slab, block)
    leaving = soap_block(
        order,
        leave,
        arrived,
        factor_left[0, 0],
        factor_right[0, 0],
        basis_left[0, 0],
        basis_right[0, 0],
        moment_first[0, 0],
        moment_second[0, 0],
    ).reshape(ring, pieces * slab, block)
    back = lax.all_to_all(leaving, "z", 0, 0, tiled=True).reshape(ring * pieces, slab, block)
    turning = pick(turn_index, back).reshape(lines, slabs * slab, block)
    returned = lax.all_to_all(turning, "x", 0, 0, tiled=True).reshape(lines * slabs, slab, block)
    spread = pick(keep_index, returned).reshape(turn, slabs * slab, block)
    return gather_columns(core, spread, (1, slabs, slab, width))


def solution(mesh):
    chips = Mesh(mesh.devices.reshape(8, 2, 4, 12), ("y", "core", "x", "z"))
    rep, own = ("y", "core"), ("x", "z")
    state = P(rep, own, None, None)
    return jax.shard_map(
        per_device,
        mesh=chips,
        in_specs=(P(rep, own, None, None, None), P()) + (state,) * 6,
        out_specs=P(own, None, None, None),
        check_vma=False,
    )
```

```python
import jax
import jax.numpy as jnp
from jax import lax
from jax.experimental import pallas as pl
from jax.experimental.pallas import tpu as pltpu
from jax.sharding import Mesh
from jax.sharding import PartitionSpec as P

BETA_ONE = 0.9
BETA_TWO = 0.95
EPSILON = 1e-08
PANEL = 128
GROUP = 8
F32 = jnp.float32
BF16 = jnp.bfloat16
NN = (((1,), (0,)), ((), ()))
NT = (((1,), (1,)), ((), ()))
TN = (((0,), (0,)), ((), ()))


def dot(a, b, dims, precision=None):
    return lax.dot_general(a, b, dims, precision=precision, preferred_element_type=F32)


def exact(a, b, dims):
    return dot(a, b, dims, lax.Precision.HIGHEST)


def times_bf16(a, b):
    high = a.astype(BF16)
    rest = a - high.astype(F32)
    middle = rest.astype(BF16)
    low = (rest - middle.astype(F32)).astype(BF16)
    return dot(low, b, NN) + dot(middle, b, NN) + dot(high, b, NN)


def three_terms(x):
    high = x.astype(BF16).astype(F32)
    middle = (x - high).astype(BF16).astype(F32)
    return high, middle, (x - high) - middle


def bf16_terms(x):
    return tuple(term.astype(BF16) for term in three_terms(x))


def down(a, b):
    total = dot(a[0], b[2], TN)
    for terms, other in ((a[:2], b[1]), (a, b[0])):
        stacked = dot(jnp.concatenate(terms, axis=1), other, TN)
        parts = [stacked[PANEL * i : PANEL * (i + 1)] for i in range(len(terms))]
        for part in reversed(parts):
            total = total + part
    return total


def across_panel(a, b, axis):
    dims = (NN, NT)[axis]
    total = None
    for i, j, k, l in ((2, 1, 0, 1), (1, 0, 0, 2), (0, 0, 0, 1)):
        product = dot(
            jnp.concatenate([a[i], a[j]], axis=1), jnp.concatenate([b[k], b[l]], axis=axis), dims
        )
        total = product if total is None else total + product
    return total


def inverse_factors(grams, spare):
    rows = PANEL // GROUP
    tile = (GROUP, PANEL)
    lane = lax.broadcasted_iota(jnp.int32, tile, 1)
    sub = lax.broadcasted_iota(jnp.int32, tile, 0)
    tiles = [[g[GROUP * r : GROUP * (r + 1), :] for r in range(rows)] for g in grams]
    for p in range(rows):
        first = GROUP * p
        in_group = (lane >= first) & (lane < first + GROUP)
        unit = jnp.where(lane == first + sub, 1.0, 0.0)
        for t, room in zip(tiles, spare):
            columns = [
                [jnp.broadcast_to(t[r][:, first + j : first + j + 1], tile) for r in range(p, min(p + 2, rows))]
                for j in range(GROUP)
            ]
            for j in range(GROUP):
                room[p, j] = columns[j][0]
            square = [
                [jnp.broadcast_to(room[p, j, i : i + 1, :], tile) if i >= j else None for j in range(GROUP)]
                for i in range(GROUP)
            ]
            scales = []
            for j in range(GROUP):
                scale = lax.rsqrt(square[j][j])
                scales.append(scale)
                for i in range(j + 1, GROUP):
                    square[i][j] = square[i][j] * scale
                for k in range(j + 1, GROUP):
                    for i in range(k, GROUP):
                        square[i][k] = square[i][k] - square[i][j] * square[k][j]
            room[p, GROUP] = jnp.where(in_group, unit, t[p])
            solved = [jnp.broadcast_to(room[p, GROUP, j : j + 1, :], tile) for j in range(GROUP)]
            for j in range(GROUP):
                solved[j] = solved[j] * scales[j]
                for i in range(j + 1, GROUP):
                    solved[i] = solved[i] - square[i][j] * solved[j]
            done = solved[0]
            for j in range(1, GROUP):
                done = jnp.where(sub == j, solved[j], done)
            t[p] = done
            if p + 1 < rows:
                below = [c[1] for c in columns]
                rest = jnp.where(in_group, 0.0, t[p + 1])
                for j in range(GROUP):
                    below[j] = below[j] * scales[j]
                    for i in range(j + 1, GROUP):
                        below[i] = below[i] - square[i][j] * below[j]
                    rest = rest - below[j] * solved[j]
                t[p + 1] = rest
            if p + 2 < rows:
                high, middle, low = three_terms(done)
                left = [jnp.where(lane >= first + 2 * GROUP, x, 0.0) for x in (high, middle, low)]
                lhs = jnp.concatenate([left[i] for i in (0, 1, 0, 2, 0, 1)], axis=0)
                rhs = jnp.concatenate([high, high, middle, high, low, middle], axis=0)
                product = dot(lhs.astype(BF16), rhs.astype(BF16), TN)
                for r in range(p + 2, rows):
                    rest = jnp.where(in_group, 0.0, t[r])
                    t[r] = rest - product[GROUP * r : GROUP * (r + 1), :]
    return [
        jnp.concatenate(
            [jnp.where(lane <= sub + GROUP * r, x, 0.0) for r, x in enumerate(t)], axis=0
        )
        for t in tiles
    ]


def block_kernel(
    order,
    slots,
    arrived,
    fl_ref,
    fr_ref,
    bl_ref,
    br_ref,
    m1_ref,
    m2_ref,
    out_ref,
    ml,
    mr,
    ql,
    qr,
    rows_ref,
    room_left,
    room_right,
):
    spare = (room_left, room_right)
    size = fl_ref.shape[0]
    slab = arrived.shape[1]
    for i in range(size // slab):
        rows_ref[i] = arrived[order[i]]
    gradient = rows_ref[...].reshape(size, size)
    left = BETA_TWO * fl_ref[...].astype(F32) + (1.0 - BETA_TWO) * dot(gradient, gradient, NT)
    right = BETA_TWO * fr_ref[...].astype(F32) + (1.0 - BETA_TWO) * dot(gradient, gradient, TN)
    ml[...] = times_bf16(left, bl_ref[...])
    mr[...] = times_bf16(right, br_ref[...])
    def step(index, carry):
        here = pl.ds(pl.multiple_of(index * PANEL, PANEL), PANEL)
        panels = [bf16_terms(m[:, here]) for m in (ml, mr)]
        inverses = inverse_factors([down(x, x) for x in panels], spare)
        for m, q, panel, inverse in zip((ml, mr), (ql, qr), panels, inverses):
            basis = across_panel(panel, bf16_terms(inverse), 1)
            q[:, here] = basis.astype(BF16)
            m[:, here] = basis
        for done in range(size // PANEL - 1):

            @pl.when(index == done)
            def _():
                rest = slice((done + 1) * PANEL, size)
                for m in (ml, mr):
                    basis = bf16_terms(m[:, done * PANEL : (done + 1) * PANEL])
                    shares = down(basis, bf16_terms(m[:, rest]))
                    m[:, rest] = m[:, rest] - across_panel(basis, bf16_terms(shares), 0)

        return carry

    lax.fori_loop(0, size // PANEL, step, 0)
    left_rotation = ql[...]
    right_rotation = qr[...]
    half = dot(left_rotation, gradient, TN).astype(BF16)
    rotated = dot(half, right_rotation, NN)
    first_new = BETA_ONE * m1_ref[...].astype(F32) + (1.0 - BETA_ONE) * rotated
    second_new = BETA_TWO * m2_ref[...].astype(F32) + (1.0 - BETA_TWO) * rotated * rotated
    direction = (first_new / (jnp.sqrt(second_new) + EPSILON)).astype(BF16)
    turned = dot(left_rotation, direction, NN).astype(BF16)
    rows_ref[...] = dot(turned, right_rotation, NT).astype(BF16).reshape(rows_ref.shape)
    for i in range(out_ref.shape[0]):
        out_ref[i] = rows_ref[slots[i]]


VMEM = pl.BlockSpec(memory_space=pltpu.VMEM)
SMEM = pl.BlockSpec(memory_space=pltpu.SMEM)
SMALL = pltpu.CompilerParams(vmem_limit_bytes=8 * 1024 * 1024)


def soap_block(order, slots, arrived, *state):
    size = state[0].shape[0]
    slab = arrived.shape[1]
    return pl.pallas_call(
        block_kernel,
        out_shape=jax.ShapeDtypeStruct((slots.shape[0], slab, size), BF16),
        in_specs=[SMEM] * 2 + [VMEM] * (1 + len(state)),
        out_specs=VMEM,
        scratch_shapes=[pltpu.VMEM((size, size), F32)] * 2
        + [pltpu.VMEM((size, size), BF16)] * 2
        + [pltpu.VMEM((size // slab, slab, size), BF16)]
        + [pltpu.VMEM((PANEL // GROUP, GROUP + 1, GROUP, PANEL), F32)] * 2,
        compiler_params=pltpu.CompilerParams(vmem_limit_bytes=32 * 1024 * 1024),
        name="soap_block",
    )(order, slots, arrived, *state)


def pick_kernel(index, source, out):
    for i in range(out.shape[0]):
        out[i] = source[index[i]]


def pick(index, source):
    return pl.pallas_call(
        pick_kernel,
        out_shape=jax.ShapeDtypeStruct(index.shape + source.shape[1:], BF16),
        in_specs=[SMEM, VMEM],
        out_specs=VMEM,
        compiler_params=SMALL,
        name="pick",
    )(index, source)


def split_kernel(core, grad, sent, kept):
    slabs, slab, _ = grad.shape
    ring, _, block = sent.shape
    for y in range(ring):
        mine = pl.ds(pl.multiple_of((2 * y + core[0]) * block, block), block)
        other = pl.ds(pl.multiple_of((2 * y + 1 - core[0]) * block, block), block)
        for r in range(slabs):
            rows = slice(r * slab, (r + 1) * slab)
            kept[y, rows, :] = grad[r, :, mine]
            sent[y, rows, :] = grad[r, :, other]


def join_kernel(core, mine_ref, other_ref, out):
    _, slabs, slab, _ = out.shape
    ring, _, block = mine_ref.shape
    for y in range(ring):
        mine = pl.ds(pl.multiple_of((2 * y + core[0]) * block, block), block)
        other = pl.ds(pl.multiple_of((2 * y + 1 - core[0]) * block, block), block)
        for r in range(slabs):
            rows = slice(r * slab, (r + 1) * slab)
            out[0, r, :, mine] = mine_ref[y, rows, :]
            out[0, r, :, other] = other_ref[y, rows, :]


def sum_kernel(parts, out):
    total = parts[0].astype(F32)
    for y in range(1, parts.shape[0]):
        total = total + parts[y].astype(F32)
    total = total.astype(BF16)
    for x in range(out.shape[0]):
        out[x] = total


def across(core):
    return [(i, 1 - i) for i in range(core)]


def reduce_columns(core, grad, block, copies):
    ring = lax.axis_size("y")
    rows = grad.shape[0] * grad.shape[1]
    split = jax.ShapeDtypeStruct((ring, rows, block), BF16)
    sent, kept = pl.pallas_call(
        split_kernel,
        out_shape=(split, split),
        in_specs=[SMEM, VMEM],
        out_specs=(VMEM, VMEM),
        compiler_params=SMALL,
        name="split",
    )(core, grad)
    received = lax.ppermute(sent, "core", across(2))
    pair_sum = (kept.astype(F32) + received.astype(F32)).astype(BF16)
    parts = lax.all_to_all(pair_sum, "y", 0, 0, tiled=True)
    return pl.pallas_call(
        sum_kernel,
        out_shape=jax.ShapeDtypeStruct((copies, rows, block), BF16),
        in_specs=[VMEM],
        out_specs=VMEM,
        compiler_params=SMALL,
        name="sum",
    )(parts)


def gather_columns(core, spread, shape):
    mine = lax.all_to_all(spread, "y", 0, 0, tiled=True)
    other = lax.ppermute(mine, "core", across(2))
    return pl.pallas_call(
        join_kernel,
        out_shape=jax.ShapeDtypeStruct(shape, BF16),
        in_specs=[SMEM, VMEM, VMEM],
        out_specs=VMEM,
        compiler_params=SMALL,
        name="join",
    )(core, mine, other)


def per_device(
    grad_partial,
    owner,
    factor_left,
    factor_right,
    basis_left,
    basis_right,
    moment_first,
    moment_second,
):
    lines, ring, turn = lax.axis_size("x"), lax.axis_size("z"), lax.axis_size("y")
    here_x, here_z = lax.axis_index("x"), lax.axis_index("z")
    core = lax.axis_index("core")
    column = lax.axis_index(("y", "core"))
    slabs, slab, width = grad_partial.shape[2:]
    block = factor_left.shape[-1]
    span = block // slab
    pieces = -(-span // ring)
    owners = lax.dynamic_slice_in_dim(owner, column, 1, 1)[:, 0]
    count = owners.shape[0]

    def block_of(place):
        mine = owners[None, :] == place[:, None]
        return jnp.sum(jnp.where(mine, jnp.arange(count, dtype=jnp.int32)[None, :], 0), axis=1)

    def owner_of(row):
        match = row[:, None] == jnp.arange(count, dtype=jnp.int32)[None, :]
        return jnp.sum(jnp.where(match, owners[None, :], 0), axis=1)

    slot = jnp.arange(ring * pieces, dtype=jnp.int32)
    slot_z, slot_b = slot // pieces, slot % pieces
    wanted = block_of(here_x * ring + slot_z)
    start = wanted // slabs * span
    rows_from = start + lax.rem(here_z - lax.rem(start, ring) + ring, ring) + ring * slot_b
    send_index = jnp.minimum(rows_from // ring, lines - 1) * slabs + wanted % slabs
    owned = block_of((here_x * ring + here_z)[None])[0]
    owned_start = owned // slabs * span
    slab_number = jnp.arange(span, dtype=jnp.int32)
    order = lax.rem(owned_start + slab_number, ring) * pieces + slab_number // ring
    leave = lax.rem(slot_z - lax.rem(owned_start, ring) + ring, ring) + ring * slot_b
    leave = jnp.minimum(leave, span - 1)
    line = jnp.arange(lines * slabs, dtype=jnp.int32)
    place = line // slabs * ring + here_z
    source = owner_of(place // span * slabs + line % slabs)
    turn_index = lax.rem(source, ring) * pieces + lax.rem(place, span) // ring
    copy = jnp.arange(turn * slabs, dtype=jnp.int32) % slabs
    here = here_x * ring + here_z
    keep_index = owner_of(here // span * slabs + copy) // ring * slabs + copy

    core = core[None].astype(jnp.int32)
    summed = reduce_columns(core, grad_partial[0, 0], block, lines)
    lined = lax.all_to_all(summed, "x", 0, 0, tiled=True).reshape(lines * slabs, slab, block)
    outgoing = pick(send_index, lined).reshape(ring, pieces * slab, block)
    arrived = lax.all_to_all(outgoing, "z", 0, 0, tiled=True).reshape(ring * pieces, slab, block)
    leaving = soap_block(
        order,
        leave,
        arrived,
        factor_left[0, 0],
        factor_right[0, 0],
        basis_left[0, 0],
        basis_right[0, 0],
        moment_first[0, 0],
        moment_second[0, 0],
    ).reshape(ring, pieces * slab, block)
    back = lax.all_to_all(leaving, "z", 0, 0, tiled=True).reshape(ring * pieces, slab, block)
    turning = pick(turn_index, back).reshape(lines, slabs * slab, block)
    returned = lax.all_to_all(turning, "x", 0, 0, tiled=True).reshape(lines * slabs, slab, block)
    spread = pick(keep_index, returned).reshape(turn, slabs * slab, block)
    return gather_columns(core, spread, (1, slabs, slab, width))


def solution(mesh):
    chips = Mesh(mesh.devices.reshape(8, 2, 4, 12), ("y", "core", "x", "z"))
    rep, own = ("y", "core"), ("x", "z")
    state = P(rep, own, None, None)
    return jax.shard_map(
        per_device,
        mesh=chips,
        in_specs=(P(rep, own, None, None, None), P()) + (state,) * 6,
        out_specs=P(own, None, None, None),
        check_vma=False,
    )
```

```python
import jax
import jax.numpy as jnp
from jax import lax
from jax.experimental import pallas as pl
from jax.experimental.pallas import tpu as pltpu
from jax.sharding import Mesh
from jax.sharding import PartitionSpec as P

BETA_ONE = 0.9
BETA_TWO = 0.95
EPSILON = 1e-08
PANEL = 128
GROUP = 8
F32 = jnp.float32
BF16 = jnp.bfloat16
NN = (((1,), (0,)), ((), ()))
NT = (((1,), (1,)), ((), ()))
TN = (((0,), (0,)), ((), ()))


def dot(a, b, dims, precision=None):
    return lax.dot_general(a, b, dims, precision=precision, preferred_element_type=F32)


def exact(a, b, dims):
    return dot(a, b, dims, lax.Precision.HIGHEST)


def times_bf16(a, b):
    high = a.astype(BF16)
    rest = a - high.astype(F32)
    middle = rest.astype(BF16)
    low = (rest - middle.astype(F32)).astype(BF16)
    return dot(low, b, NN) + dot(middle, b, NN) + dot(high, b, NN)


def three_terms(x):
    high = x.astype(BF16).astype(F32)
    middle = (x - high).astype(BF16).astype(F32)
    return high, middle, (x - high) - middle


def bf16_terms(x):
    return tuple(term.astype(BF16) for term in three_terms(x))


def down(a, b):
    total = dot(a[0], b[2], TN)
    for terms, other in ((a[:2], b[1]), (a, b[0])):
        stacked = dot(jnp.concatenate(terms, axis=1), other, TN)
        parts = [stacked[PANEL * i : PANEL * (i + 1)] for i in range(len(terms))]
        for part in reversed(parts):
            total = total + part
    return total


def across_panel(a, b, axis):
    dims = (NN, NT)[axis]
    total = None
    for i, j, k, l in ((2, 1, 0, 1), (1, 0, 0, 2), (0, 0, 0, 1)):
        product = dot(
            jnp.concatenate([a[i], a[j]], axis=1), jnp.concatenate([b[k], b[l]], axis=axis), dims
        )
        total = product if total is None else total + product
    return total


def inverse_factors(grams, spare):
    rows = PANEL // GROUP
    tile = (GROUP, PANEL)
    lane = lax.broadcasted_iota(jnp.int32, tile, 1)
    sub = lax.broadcasted_iota(jnp.int32, tile, 0)
    tiles = [[g[GROUP * r : GROUP * (r + 1), :] for r in range(rows)] for g in grams]
    pair_lane = lax.broadcasted_iota(jnp.int32, (2 * GROUP, PANEL), 1)
    kept = []
    for p in range(rows):
        first = GROUP * p
        in_group = (lane >= first) & (lane < first + GROUP)
        unit = jnp.where(lane == first + sub, 1.0, 0.0)
        for t, room in zip(tiles, spare):
            columns = [
                [jnp.broadcast_to(t[r][:, first + j : first + j + 1], tile) for r in range(p, min(p + 4 - p % 2, rows))]
                for j in range(GROUP)
            ]
            for j in range(GROUP):
                room[p, j] = columns[j][0]
            square = [
                [jnp.broadcast_to(room[p, j, i : i + 1, :], tile) if i >= j else None for j in range(GROUP)]
                for i in range(GROUP)
            ]
            scales = []
            for j in range(GROUP):
                scale = lax.rsqrt(square[j][j])
                scales.append(scale)
                for i in range(j + 1, GROUP):
                    square[i][j] = square[i][j] * scale
                for k in range(j + 1, GROUP):
                    for i in range(k, GROUP):
                        square[i][k] = square[i][k] - square[i][j] * square[k][j]
            room[p, GROUP] = jnp.where(in_group, unit, t[p])
            solved = [jnp.broadcast_to(room[p, GROUP, j : j + 1, :], tile) for j in range(GROUP)]
            for j in range(GROUP):
                solved[j] = solved[j] * scales[j]
                for i in range(j + 1, GROUP):
                    solved[i] = solved[i] - square[i][j] * solved[j]
            done = solved[0]
            for j in range(1, GROUP):
                done = jnp.where(sub == j, solved[j], done)
            t[p] = done
            for r in range(p + 1, min(p + 4 - p % 2, rows)):
                below = [c[r - p] for c in columns]
                rest = jnp.where(in_group, 0.0, t[r])
                for j in range(GROUP):
                    below[j] = below[j] * scales[j]
                    for i in range(j + 1, GROUP):
                        below[i] = below[i] - square[i][j] * below[j]
                    rest = rest - below[j] * solved[j]
                t[r] = rest
            last = p - p % 2 + 4
            if p % 2 == 0 and last < rows:
                ahead = (lane >= first + GROUP) & (lane < first + 2 * GROUP)
                kept.append(jnp.where(ahead, 0.0, done))
            elif p % 2 == 1 and last < rows:
                pair = jnp.concatenate([kept.pop(0), done], axis=0)
                high, middle, low = three_terms(pair)
                left = [jnp.where(pair_lane >= last * GROUP, x, 0.0) for x in (high, middle, low)]
                lhs = jnp.concatenate([left[i] for i in (0, 1, 0, 2, 0, 1)], axis=0)
                rhs = jnp.concatenate([high, high, middle, high, low, middle], axis=0)
                product = dot(lhs.astype(BF16), rhs.astype(BF16), TN)
                in_pair = (lane >= first - GROUP) & (lane < first + GROUP)
                for r in range(last, rows):
                    rest = jnp.where(in_pair, 0.0, t[r])
                    t[r] = rest - product[GROUP * r : GROUP * (r + 1), :]
    return [
        jnp.concatenate(
            [jnp.where(lane <= sub + GROUP * r, x, 0.0) for r, x in enumerate(t)], axis=0
        )
        for t in tiles
    ]


def block_kernel(
    order,
    slots,
    arrived,
    fl_ref,
    fr_ref,
    bl_ref,
    br_ref,
    m1_ref,
    m2_ref,
    out_ref,
    ml,
    mr,
    ql,
    qr,
    rows_ref,
    room_left,
    room_right,
):
    spare = (room_left, room_right)
    size = fl_ref.shape[0]
    slab = arrived.shape[1]
    for i in range(size // slab):
        rows_ref[i] = arrived[order[i]]
    gradient = rows_ref[...].reshape(size, size)
    left = BETA_TWO * fl_ref[...].astype(F32) + (1.0 - BETA_TWO) * dot(gradient, gradient, NT)
    right = BETA_TWO * fr_ref[...].astype(F32) + (1.0 - BETA_TWO) * dot(gradient, gradient, TN)
    ml[...] = times_bf16(left, bl_ref[...])
    mr[...] = times_bf16(right, br_ref[...])
    def step(index, carry):
        here = pl.ds(pl.multiple_of(index * PANEL, PANEL), PANEL)
        panels = [bf16_terms(m[:, here]) for m in (ml, mr)]
        inverses = inverse_factors([down(x, x) for x in panels], spare)
        for m, q, panel, inverse in zip((ml, mr), (ql, qr), panels, inverses):
            basis = across_panel(panel, bf16_terms(inverse), 1)
            q[:, here] = basis.astype(BF16)
            m[:, here] = basis
        for done in range(size // PANEL - 1):

            @pl.when(index == done)
            def _():
                rest = slice((done + 1) * PANEL, size)
                for m in (ml, mr):
                    basis = bf16_terms(m[:, done * PANEL : (done + 1) * PANEL])
                    shares = down(basis, bf16_terms(m[:, rest]))
                    m[:, rest] = m[:, rest] - across_panel(basis, bf16_terms(shares), 0)

        return carry

    lax.fori_loop(0, size // PANEL, step, 0)
    left_rotation = ql[...]
    right_rotation = qr[...]
    half = dot(left_rotation, gradient, TN).astype(BF16)
    rotated = dot(half, right_rotation, NN)
    first_new = BETA_ONE * m1_ref[...].astype(F32) + (1.0 - BETA_ONE) * rotated
    second_new = BETA_TWO * m2_ref[...].astype(F32) + (1.0 - BETA_TWO) * rotated * rotated
    direction = (first_new / (jnp.sqrt(second_new) + EPSILON)).astype(BF16)
    turned = dot(left_rotation, direction, NN).astype(BF16)
    rows_ref[...] = dot(turned, right_rotation, NT).astype(BF16).reshape(rows_ref.shape)
    for i in range(out_ref.shape[0]):
        out_ref[i] = rows_ref[slots[i]]


VMEM = pl.BlockSpec(memory_space=pltpu.VMEM)
SMEM = pl.BlockSpec(memory_space=pltpu.SMEM)
SMALL = pltpu.CompilerParams(vmem_limit_bytes=8 * 1024 * 1024)


def soap_block(order, slots, arrived, *state):
    size = state[0].shape[0]
    slab = arrived.shape[1]
    return pl.pallas_call(
        block_kernel,
        out_shape=jax.ShapeDtypeStruct((slots.shape[0], slab, size), BF16),
        in_specs=[SMEM] * 2 + [VMEM] * (1 + len(state)),
        out_specs=VMEM,
        scratch_shapes=[pltpu.VMEM((size, size), F32)] * 2
        + [pltpu.VMEM((size, size), BF16)] * 2
        + [pltpu.VMEM((size // slab, slab, size), BF16)]
        + [pltpu.VMEM((PANEL // GROUP, GROUP + 1, GROUP, PANEL), F32)] * 2,
        compiler_params=pltpu.CompilerParams(vmem_limit_bytes=32 * 1024 * 1024),
        name="soap_block",
    )(order, slots, arrived, *state)


def pick_kernel(index, source, out):
    for i in range(out.shape[0]):
        out[i] = source[index[i]]


def pick(index, source):
    return pl.pallas_call(
        pick_kernel,
        out_shape=jax.ShapeDtypeStruct(index.shape + source.shape[1:], BF16),
        in_specs=[SMEM, VMEM],
        out_specs=VMEM,
        compiler_params=SMALL,
        name="pick",
    )(index, source)


def split_kernel(core, grad, sent, kept):
    slabs, slab, _ = grad.shape
    ring, _, block = sent.shape
    for y in range(ring):
        mine = pl.ds(pl.multiple_of((2 * y + core[0]) * block, block), block)
        other = pl.ds(pl.multiple_of((2 * y + 1 - core[0]) * block, block), block)
        for r in range(slabs):
            rows = slice(r * slab, (r + 1) * slab)
            kept[y, rows, :] = grad[r, :, mine]
            sent[y, rows, :] = grad[r, :, other]


def join_kernel(core, mine_ref, other_ref, out):
    _, slabs, slab, _ = out.shape
    ring, _, block = mine_ref.shape
    for y in range(ring):
        mine = pl.ds(pl.multiple_of((2 * y + core[0]) * block, block), block)
        other = pl.ds(pl.multiple_of((2 * y + 1 - core[0]) * block, block), block)
        for r in range(slabs):
            rows = slice(r * slab, (r + 1) * slab)
            out[0, r, :, mine] = mine_ref[y, rows, :]
            out[0, r, :, other] = other_ref[y, rows, :]


def sum_kernel(parts, out):
    total = parts[0].astype(F32)
    for y in range(1, parts.shape[0]):
        total = total + parts[y].astype(F32)
    total = total.astype(BF16)
    for x in range(out.shape[0]):
        out[x] = total


def across(core):
    return [(i, 1 - i) for i in range(core)]


def reduce_columns(core, grad, block, copies):
    ring = lax.axis_size("y")
    rows = grad.shape[0] * grad.shape[1]
    split = jax.ShapeDtypeStruct((ring, rows, block), BF16)
    sent, kept = pl.pallas_call(
        split_kernel,
        out_shape=(split, split),
        in_specs=[SMEM, VMEM],
        out_specs=(VMEM, VMEM),
        compiler_params=SMALL,
        name="split",
    )(core, grad)
    received = lax.ppermute(sent, "core", across(2))
    pair_sum = (kept.astype(F32) + received.astype(F32)).astype(BF16)
    parts = lax.all_to_all(pair_sum, "y", 0, 0, tiled=True)
    return pl.pallas_call(
        sum_kernel,
        out_shape=jax.ShapeDtypeStruct((copies, rows, block), BF16),
        in_specs=[VMEM],
        out_specs=VMEM,
        compiler_params=SMALL,
        name="sum",
    )(parts)


def gather_columns(core, spread, shape):
    mine = lax.all_to_all(spread, "y", 0, 0, tiled=True)
    other = lax.ppermute(mine, "core", across(2))
    return pl.pallas_call(
        join_kernel,
        out_shape=jax.ShapeDtypeStruct(shape, BF16),
        in_specs=[SMEM, VMEM, VMEM],
        out_specs=VMEM,
        compiler_params=SMALL,
        name="join",
    )(core, mine, other)


def per_device(
    grad_partial,
    owner,
    factor_left,
    factor_right,
    basis_left,
    basis_right,
    moment_first,
    moment_second,
):
    lines, ring, turn = lax.axis_size("x"), lax.axis_size("z"), lax.axis_size("y")
    here_x, here_z = lax.axis_index("x"), lax.axis_index("z")
    core = lax.axis_index("core")
    column = lax.axis_index(("y", "core"))
    slabs, slab, width = grad_partial.shape[2:]
    block = factor_left.shape[-1]
    span = block // slab
    pieces = -(-span // ring)
    owners = lax.dynamic_slice_in_dim(owner, column, 1, 1)[:, 0]
    count = owners.shape[0]

    def block_of(place):
        mine = owners[None, :] == place[:, None]
        return jnp.sum(jnp.where(mine, jnp.arange(count, dtype=jnp.int32)[None, :], 0), axis=1)

    def owner_of(row):
        match = row[:, None] == jnp.arange(count, dtype=jnp.int32)[None, :]
        return jnp.sum(jnp.where(match, owners[None, :], 0), axis=1)

    slot = jnp.arange(ring * pieces, dtype=jnp.int32)
    slot_z, slot_b = slot // pieces, slot % pieces
    wanted = block_of(here_x * ring + slot_z)
    start = wanted // slabs * span
    rows_from = start + lax.rem(here_z - lax.rem(start, ring) + ring, ring) + ring * slot_b
    send_index = jnp.minimum(rows_from // ring, lines - 1) * slabs + wanted % slabs
    owned = block_of((here_x * ring + here_z)[None])[0]
    owned_start = owned // slabs * span
    slab_number = jnp.arange(span, dtype=jnp.int32)
    order = lax.rem(owned_start + slab_number, ring) * pieces + slab_number // ring
    leave = lax.rem(slot_z - lax.rem(owned_start, ring) + ring, ring) + ring * slot_b
    leave = jnp.minimum(leave, span - 1)
    line = jnp.arange(lines * slabs, dtype=jnp.int32)
    place = line // slabs * ring + here_z
    source = owner_of(place // span * slabs + line % slabs)
    turn_index = lax.rem(source, ring) * pieces + lax.rem(place, span) // ring
    copy = jnp.arange(turn * slabs, dtype=jnp.int32) % slabs
    here = here_x * ring + here_z
    keep_index = owner_of(here // span * slabs + copy) // ring * slabs + copy

    core = core[None].astype(jnp.int32)
    summed = reduce_columns(core, grad_partial[0, 0], block, lines)
    lined = lax.all_to_all(summed, "x", 0, 0, tiled=True).reshape(lines * slabs, slab, block)
    outgoing = pick(send_index, lined).reshape(ring, pieces * slab, block)
    arrived = lax.all_to_all(outgoing, "z", 0, 0, tiled=True).reshape(ring * pieces, slab, block)
    leaving = soap_block(
        order,
        leave,
        arrived,
        factor_left[0, 0],
        factor_right[0, 0],
        basis_left[0, 0],
        basis_right[0, 0],
        moment_first[0, 0],
        moment_second[0, 0],
    ).reshape(ring, pieces * slab, block)
    back = lax.all_to_all(leaving, "z", 0, 0, tiled=True).reshape(ring * pieces, slab, block)
    turning = pick(turn_index, back).reshape(lines, slabs * slab, block)
    returned = lax.all_to_all(turning, "x", 0, 0, tiled=True).reshape(lines * slabs, slab, block)
    spread = pick(keep_index, returned).reshape(turn, slabs * slab, block)
    return gather_columns(core, spread, (1, slabs, slab, width))


def solution(mesh):
    chips = Mesh(mesh.devices.reshape(8, 2, 4, 12), ("y", "core", "x", "z"))
    rep, own = ("y", "core"), ("x", "z")
    state = P(rep, own, None, None)
    return jax.shard_map(
        per_device,
        mesh=chips,
        in_specs=(P(rep, own, None, None, None), P()) + (state,) * 6,
        out_specs=P(own, None, None, None),
        check_vma=False,
    )
```

```python
import jax
import jax.numpy as jnp
from jax import lax
from jax.experimental import pallas as pl
from jax.experimental.pallas import tpu as pltpu
from jax.sharding import Mesh
from jax.sharding import PartitionSpec as P

BETA_ONE = 0.9
BETA_TWO = 0.95
EPSILON = 1e-08
PANEL = 128
GROUP = 8
F32 = jnp.float32
BF16 = jnp.bfloat16
NN = (((1,), (0,)), ((), ()))
NT = (((1,), (1,)), ((), ()))
TN = (((0,), (0,)), ((), ()))


def dot(a, b, dims, precision=None):
    return lax.dot_general(a, b, dims, precision=precision, preferred_element_type=F32)


def exact(a, b, dims):
    return dot(a, b, dims, lax.Precision.HIGHEST)


def times_bf16(a, b):
    high = a.astype(BF16)
    rest = a - high.astype(F32)
    middle = rest.astype(BF16)
    low = (rest - middle.astype(F32)).astype(BF16)
    return dot(low, b, NN) + dot(middle, b, NN) + dot(high, b, NN)


def three_terms(x):
    high = x.astype(BF16).astype(F32)
    middle = (x - high).astype(BF16).astype(F32)
    return high, middle, (x - high) - middle


def bf16_terms(x):
    return tuple(term.astype(BF16) for term in three_terms(x))


def down(a, b):
    total = dot(a[0], b[2], TN)
    for terms, other in ((a[:2], b[1]), (a, b[0])):
        stacked = dot(jnp.concatenate(terms, axis=1), other, TN)
        parts = [stacked[PANEL * i : PANEL * (i + 1)] for i in range(len(terms))]
        for part in reversed(parts):
            total = total + part
    return total


def across_panel(a, b, axis):
    dims = (NN, NT)[axis]
    total = None
    for i, j, k, l in ((2, 1, 0, 1), (1, 0, 0, 2), (0, 0, 0, 1)):
        product = dot(
            jnp.concatenate([a[i], a[j]], axis=1), jnp.concatenate([b[k], b[l]], axis=axis), dims
        )
        total = product if total is None else total + product
    return total


def inverse_factors(grams, spare):
    rows = PANEL // GROUP
    tile = (GROUP, PANEL)
    lane = lax.broadcasted_iota(jnp.int32, tile, 1)
    sub = lax.broadcasted_iota(jnp.int32, tile, 0)
    tiles = [[g[GROUP * r : GROUP * (r + 1), :] for r in range(rows)] for g in grams]
    pair_lane = lax.broadcasted_iota(jnp.int32, (2 * GROUP, PANEL), 1)
    kept = []
    for p in range(rows):
        first = GROUP * p
        in_group = (lane >= first) & (lane < first + GROUP)
        unit = jnp.where(lane == first + sub, 1.0, 0.0)
        for t, room in zip(tiles, spare):
            columns = [
                [jnp.broadcast_to(t[r][:, first + j : first + j + 1], tile) for r in range(p, min(p + 4 - p % 2, rows))]
                for j in range(GROUP)
            ]
            for j in range(GROUP):
                room[p, j] = columns[j][0]
            square = [
                [jnp.broadcast_to(room[p, j, i : i + 1, :], tile) if i >= j else None for j in range(GROUP)]
                for i in range(GROUP)
            ]
            scales = []
            for j in range(GROUP):
                scale = lax.rsqrt(square[j][j])
                scales.append(scale)
                for i in range(j + 1, GROUP):
                    square[i][j] = square[i][j] * scale
                for k in range(j + 1, GROUP):
                    for i in range(k, GROUP):
                        square[i][k] = square[i][k] - square[i][j] * square[k][j]
            room[p, GROUP] = jnp.where(in_group, unit, t[p])
            solved = [jnp.broadcast_to(room[p, GROUP, j : j + 1, :], tile) for j in range(GROUP)]
            for j in range(GROUP):
                solved[j] = solved[j] * scales[j]
                for i in range(j + 1, GROUP):
                    solved[i] = solved[i] - square[i][j] * solved[j]
            done = solved[0]
            for j in range(1, GROUP):
                done = jnp.where(sub == j, solved[j], done)
            t[p] = done
            for r in range(p + 1, min(p + 4 - p % 2, rows)):
                below = [c[r - p] for c in columns]
                rest = jnp.where(in_group, 0.0, t[r])
                for j in range(GROUP):
                    below[j] = below[j] * scales[j]
                    for i in range(j + 1, GROUP):
                        below[i] = below[i] - square[i][j] * below[j]
                    rest = rest - below[j] * solved[j]
                t[r] = rest
            last = p - p % 2 + 4
            if p % 2 == 0 and last < rows:
                ahead = (lane >= first + GROUP) & (lane < first + 2 * GROUP)
                kept.append(jnp.where(ahead, 0.0, done))
            elif p % 2 == 1 and last < rows:
                pair = jnp.concatenate([kept.pop(0), done], axis=0)
                high, middle, low = three_terms(pair)
                left = [jnp.where(pair_lane >= last * GROUP, x, 0.0) for x in (high, middle, low)]
                lhs = jnp.concatenate([left[i] for i in (0, 1, 0, 2, 0, 1)], axis=0)
                rhs = jnp.concatenate([high, high, middle, high, low, middle], axis=0)
                product = dot(lhs.astype(BF16), rhs.astype(BF16), TN)
                in_pair = (lane >= first - GROUP) & (lane < first + GROUP)
                for r in range(last, rows):
                    rest = jnp.where(in_pair, 0.0, t[r])
                    t[r] = rest - product[GROUP * r : GROUP * (r + 1), :]
    return [
        jnp.concatenate(
            [jnp.where(lane <= sub + GROUP * r, x, 0.0) for r, x in enumerate(t)], axis=0
        )
        for t in tiles
    ]


def block_kernel(
    order,
    slots,
    arrived,
    fl_ref,
    fr_ref,
    bl_ref,
    br_ref,
    m1_ref,
    m2_ref,
    out_ref,
    ml,
    mr,
    ql,
    qr,
    rows_ref,
    room_left,
    room_right,
):
    spare = (room_left, room_right)
    size = fl_ref.shape[0]
    slab = arrived.shape[1]
    for i in range(size // slab):
        rows_ref[i] = arrived[order[i]]
    gradient = rows_ref[...].reshape(size, size)
    left = BETA_TWO * fl_ref[...].astype(F32) + (1.0 - BETA_TWO) * dot(gradient, gradient, NT)
    right = BETA_TWO * fr_ref[...].astype(F32) + (1.0 - BETA_TWO) * dot(gradient, gradient, TN)
    ml[...] = times_bf16(left, bl_ref[...])
    mr[...] = times_bf16(right, br_ref[...])
    def step(index, carry):
        here = pl.ds(pl.multiple_of(index * PANEL, PANEL), PANEL)
        panels = [bf16_terms(m[:, here]) for m in (ml, mr)]
        inverses = inverse_factors([down(x, x) for x in panels], spare)
        for m, q, panel, inverse in zip((ml, mr), (ql, qr), panels, inverses):
            basis = across_panel(panel, bf16_terms(inverse), 1)
            q[:, here] = basis.astype(BF16)
            m[:, here] = basis
        for done in range(size // PANEL - 1):

            @pl.when(index == done)
            def _():
                rest = slice((done + 1) * PANEL, size)
                for m in (ml, mr):
                    basis = bf16_terms(m[:, done * PANEL : (done + 1) * PANEL])
                    shares = down(basis, bf16_terms(m[:, rest]))
                    m[:, rest] = m[:, rest] - across_panel(basis, bf16_terms(shares), 0)

        return carry

    lax.fori_loop(0, size // PANEL, step, 0)
    left_rotation = ql[...]
    right_rotation = qr[...]
    half = dot(left_rotation, gradient, TN).astype(BF16)
    rotated = dot(half, right_rotation, NN)
    first_new = BETA_ONE * m1_ref[...].astype(F32) + (1.0 - BETA_ONE) * rotated
    second_new = BETA_TWO * m2_ref[...].astype(F32) + (1.0 - BETA_TWO) * rotated * rotated
    direction = (first_new / (jnp.sqrt(second_new) + EPSILON)).astype(BF16)
    turned = dot(left_rotation, direction, NN).astype(BF16)
    rows_ref[...] = dot(turned, right_rotation, NT).astype(BF16).reshape(rows_ref.shape)
    for i in range(out_ref.shape[0]):
        out_ref[i] = rows_ref[slots[i]]


VMEM = pl.BlockSpec(memory_space=pltpu.VMEM)
SMEM = pl.BlockSpec(memory_space=pltpu.SMEM)
SMALL = pltpu.CompilerParams(vmem_limit_bytes=8 * 1024 * 1024)


def soap_block(order, slots, arrived, *state):
    size = state[0].shape[0]
    slab = arrived.shape[1]
    return pl.pallas_call(
        block_kernel,
        out_shape=jax.ShapeDtypeStruct((slots.shape[0], slab, size), BF16),
        in_specs=[SMEM] * 2 + [VMEM] * (1 + len(state)),
        out_specs=VMEM,
        scratch_shapes=[pltpu.VMEM((size, size), F32)] * 2
        + [pltpu.VMEM((size, size), BF16)] * 2
        + [pltpu.VMEM((size // slab, slab, size), BF16)]
        + [pltpu.VMEM((PANEL // GROUP, GROUP + 1, GROUP, PANEL), F32)] * 2,
        compiler_params=pltpu.CompilerParams(vmem_limit_bytes=24 * 1024 * 1024),
        name="soap_block",
    )(order, slots, arrived, *state)


def pick_kernel(index, source, out):
    for i in range(out.shape[0]):
        out[i] = source[index[i]]


def pick(index, source):
    return pl.pallas_call(
        pick_kernel,
        out_shape=jax.ShapeDtypeStruct(index.shape + source.shape[1:], BF16),
        in_specs=[SMEM, VMEM],
        out_specs=VMEM,
        compiler_params=SMALL,
        name="pick",
    )(index, source)


def split_kernel(core, grad, sent, kept):
    slabs, slab, _ = grad.shape
    ring, _, block = sent.shape
    for y in range(ring):
        mine = pl.ds(pl.multiple_of((2 * y + core[0]) * block, block), block)
        other = pl.ds(pl.multiple_of((2 * y + 1 - core[0]) * block, block), block)
        for r in range(slabs):
            rows = slice(r * slab, (r + 1) * slab)
            kept[y, rows, :] = grad[r, :, mine]
            sent[y, rows, :] = grad[r, :, other]


def join_kernel(core, mine_ref, other_ref, out):
    _, slabs, slab, _ = out.shape
    ring, _, block = mine_ref.shape
    for y in range(ring):
        mine = pl.ds(pl.multiple_of((2 * y + core[0]) * block, block), block)
        other = pl.ds(pl.multiple_of((2 * y + 1 - core[0]) * block, block), block)
        for r in range(slabs):
            rows = slice(r * slab, (r + 1) * slab)
            out[0, r, :, mine] = mine_ref[y, rows, :]
            out[0, r, :, other] = other_ref[y, rows, :]


def sum_kernel(parts, out):
    total = parts[0].astype(F32)
    for y in range(1, parts.shape[0]):
        total = total + parts[y].astype(F32)
    total = total.astype(BF16)
    for x in range(out.shape[0]):
        out[x] = total


def across(core):
    return [(i, 1 - i) for i in range(core)]


def reduce_columns(core, grad, block, copies):
    ring = lax.axis_size("y")
    rows = grad.shape[0] * grad.shape[1]
    split = jax.ShapeDtypeStruct((ring, rows, block), BF16)
    sent, kept = pl.pallas_call(
        split_kernel,
        out_shape=(split, split),
        in_specs=[SMEM, VMEM],
        out_specs=(VMEM, VMEM),
        compiler_params=SMALL,
        name="split",
    )(core, grad)
    received = lax.ppermute(sent, "core", across(2))
    pair_sum = (kept.astype(F32) + received.astype(F32)).astype(BF16)
    parts = lax.all_to_all(pair_sum, "y", 0, 0, tiled=True)
    return pl.pallas_call(
        sum_kernel,
        out_shape=jax.ShapeDtypeStruct((copies, rows, block), BF16),
        in_specs=[VMEM],
        out_specs=VMEM,
        compiler_params=SMALL,
        name="sum",
    )(parts)


def gather_columns(core, spread, shape):
    mine = lax.all_to_all(spread, "y", 0, 0, tiled=True)
    other = lax.ppermute(mine, "core", across(2))
    return pl.pallas_call(
        join_kernel,
        out_shape=jax.ShapeDtypeStruct(shape, BF16),
        in_specs=[SMEM, VMEM, VMEM],
        out_specs=VMEM,
        compiler_params=SMALL,
        name="join",
    )(core, mine, other)


def per_device(
    grad_partial,
    owner,
    factor_left,
    factor_right,
    basis_left,
    basis_right,
    moment_first,
    moment_second,
):
    lines, ring, turn = lax.axis_size("x"), lax.axis_size("z"), lax.axis_size("y")
    here_x, here_z = lax.axis_index("x"), lax.axis_index("z")
    core = lax.axis_index("core")
    column = lax.axis_index(("y", "core"))
    slabs, slab, width = grad_partial.shape[2:]
    block = factor_left.shape[-1]
    span = block // slab
    pieces = -(-span // ring)
    owners = lax.dynamic_slice_in_dim(owner, column, 1, 1)[:, 0]
    count = owners.shape[0]

    def block_of(place):
        mine = owners[None, :] == place[:, None]
        return jnp.sum(jnp.where(mine, jnp.arange(count, dtype=jnp.int32)[None, :], 0), axis=1)

    def owner_of(row):
        match = row[:, None] == jnp.arange(count, dtype=jnp.int32)[None, :]
        return jnp.sum(jnp.where(match, owners[None, :], 0), axis=1)

    slot = jnp.arange(ring * pieces, dtype=jnp.int32)
    slot_z, slot_b = slot // pieces, slot % pieces
    wanted = block_of(here_x * ring + slot_z)
    start = wanted // slabs * span
    rows_from = start + lax.rem(here_z - lax.rem(start, ring) + ring, ring) + ring * slot_b
    send_index = jnp.minimum(rows_from // ring, lines - 1) * slabs + wanted % slabs
    owned = block_of((here_x * ring + here_z)[None])[0]
    owned_start = owned // slabs * span
    slab_number = jnp.arange(span, dtype=jnp.int32)
    order = lax.rem(owned_start + slab_number, ring) * pieces + slab_number // ring
    leave = lax.rem(slot_z - lax.rem(owned_start, ring) + ring, ring) + ring * slot_b
    leave = jnp.minimum(leave, span - 1)
    line = jnp.arange(lines * slabs, dtype=jnp.int32)
    place = line // slabs * ring + here_z
    source = owner_of(place // span * slabs + line % slabs)
    turn_index = lax.rem(source, ring) * pieces + lax.rem(place, span) // ring
    copy = jnp.arange(turn * slabs, dtype=jnp.int32) % slabs
    here = here_x * ring + here_z
    keep_index = owner_of(here // span * slabs + copy) // ring * slabs + copy

    core = core[None].astype(jnp.int32)
    summed = reduce_columns(core, grad_partial[0, 0], block, lines)
    lined = lax.all_to_all(summed, "x", 0, 0, tiled=True).reshape(lines * slabs, slab, block)
    outgoing = pick(send_index, lined).reshape(ring, pieces * slab, block)
    arrived = lax.all_to_all(outgoing, "z", 0, 0, tiled=True).reshape(ring * pieces, slab, block)
    leaving = soap_block(
        order,
        leave,
        arrived,
        factor_left[0, 0],
        factor_right[0, 0],
        basis_left[0, 0],
        basis_right[0, 0],
        moment_first[0, 0],
        moment_second[0, 0],
    ).reshape(ring, pieces * slab, block)
    back = lax.all_to_all(leaving, "z", 0, 0, tiled=True).reshape(ring * pieces, slab, block)
    turning = pick(turn_index, back).reshape(lines, slabs * slab, block)
    returned = lax.all_to_all(turning, "x", 0, 0, tiled=True).reshape(lines * slabs, slab, block)
    spread = pick(keep_index, returned).reshape(turn, slabs * slab, block)
    return gather_columns(core, spread, (1, slabs, slab, width))


def solution(mesh):
    chips = Mesh(mesh.devices.reshape(8, 2, 4, 12), ("y", "core", "x", "z"))
    rep, own = ("y", "core"), ("x", "z")
    state = P(rep, own, None, None)
    return jax.shard_map(
        per_device,
        mesh=chips,
        in_specs=(P(rep, own, None, None, None), P()) + (state,) * 6,
        out_specs=P(own, None, None, None),
        check_vma=False,
    )
```
